32 devices in a mesh: groups: 2 (over y), tm: 8 (over z, x), head: 2 (over core).
Axes of the slice: x: 2, y: 2, z: 4, core: 2. Of those that a mesh axis runs over, the one named last changes fastest.
Arguments:
- queries: bfloat16 [4096, 2560], P(('groups', 'tm'), 'head'), parts along dimension 0, may hold values from -2.5 to 2.5
- keys: bfloat16 [4096, 2560], P(('groups', 'tm'), 'head'), parts along dimension 0, may hold values from -2.5 to 2.5
- values: bfloat16 [4096, 2560], P(('groups', 'tm'), 'head'), parts along dimension 0, may hold values from -6 to 6
- out_grad: bfloat16 [4096, 2560], P(('groups', 'tm'), 'head'), parts along dimension 0, may hold values from -6 to 6
- pair_mask: int32 [16, 5], P('groups'), parts along dimension 0, may hold values from 0 to 1, as said below
Outputs:
- query_grad: bfloat16 [4096, 2560], P(('groups', 'tm'), 'head'), parts along dimension 0
- key_grad: bfloat16 [4096, 2560], P(('groups', 'tm'), 'head'), parts along dimension 0
- value_grad: bfloat16 [4096, 2560], P(('groups', 'tm'), 'head'), parts along dimension 0
The draws below stay inside these ranges and needn't reach their ends.
There are 2 independent parts, one for each index of `groups`. The reference program is written for one: setup_inputs(seed, part) draws one part's arguments, and reference() takes and returns one part's arrays. A program takes and returns all parts, laid end to end along the dimension named above; each array names one. Nothing has to cross between parts.
Inputs may be any that keep to these rules, and one draw needn't show every extreme that they name: pair_mask[f, s] is 1 where query frame f attends the key frame of slot s. It is 1 for slot 0 and for offsets 1 and -1 wherever the key frame lies inside the video, and 0 wherever the key frame lies outside it.
All inputs are finite; a program needn't handle non-finite values.
Results may differ from the reference program's by a relative error of at most 0.0062.
Values may be sent and summed in bfloat16 or wider, within the bound.
A program may use at most 64 MiB of HBM per device.

```python
import jax
import jax.numpy as jnp
from jax import lax

FTOK = 256
HEADS = 20
HDIM = 128
DISTANCE_LEVELS = 2
VIDEO_FRAMES = 8
TOKENS = 2048
KEY_SLOTS = 5


def draw_pair_mask(key, part):
    key = jax.random.fold_in(key, 7)
    offset_list = [0]
    level_list = [0]
    for level_index in range(DISTANCE_LEVELS):
        offset_list = offset_list + [2 ** level_index, -2 ** level_index]
        level_list = level_list + [level_index, level_index]
    offsets = jnp.array(offset_list, jnp.int32)
    level_table = jnp.array(level_list, jnp.int32)
    frame_rolls = jax.random.randint(key, (VIDEO_FRAMES, KEY_SLOTS), 0, 2 ** DISTANCE_LEVELS)
    keep = frame_rolls % jnp.left_shift(1, level_table)[None, :] == 0
    target = jnp.arange(VIDEO_FRAMES, dtype=jnp.int32)[:, None] + offsets[None, :]
    within_frame = (target >= 0) & (target < VIDEO_FRAMES)
    return (keep & within_frame).astype(jnp.int32)


def block_levels(own_key, extent, split, least, top_value):
    def one(axis_at, shards_of):
        steps = jax.random.uniform(jax.random.fold_in(jax.random.fold_in(own_key, 6), axis_at), (shards_of,), jnp.float32, least / len(split), top_value / len(split))
        return jnp.repeat(jnp.exp(steps), extent[axis_at] // shards_of).reshape((-1,) + (1,) * (len(extent) - axis_at - 1))

    level = one(*split[0])
    for cut in split[1:]:
        level = level * one(*cut)
    return level


def gaussian(key, dims, deviation, bound, shards=(), held_as=jnp.bfloat16):
    drawn = jax.random.normal(key, dims, jnp.float32) * deviation
    if len(shards) > 0:
        drawn = block_levels(key, dims, shards, -0.22, 0.18) * drawn
    return jnp.clip(drawn, min=-bound, max=bound).astype(held_as)


def setup_inputs(seed: int = 0, part: int = 0) -> dict:
    splits = jax.random.split(jax.random.key(seed), 6)
    own_keys = jax.random.split(jax.random.fold_in(splits[5], part), 6)
    return {
        "queries": gaussian(own_keys[0], (TOKENS, HEADS * HDIM), 1.0, 2.5, ((0, 8), (1, 2))),
        "keys": gaussian(own_keys[1], (TOKENS, HEADS * HDIM), 1.0, 2.5, ((0, 8), (1, 2))),
        "values": gaussian(own_keys[2], (TOKENS, HEADS * HDIM), 1.0, 6.0, ((0, 8), (1, 2))),
        "out_grad": gaussian(own_keys[3], (TOKENS, HEADS * HDIM), 1.0, 6.0, ((0, 8), (1, 2))),
        "pair_mask": draw_pair_mask(jax.random.fold_in(jax.random.fold_in(splits[5], part), 71), part),
    }


def slot_offsets(levels):
    offsets = [0]
    for level_index in range(levels):
        offsets = offsets + [2 ** level_index, -(2 ** level_index)]
    return offsets


def frame_shifted(array, offset):
    count = array.shape[0]
    padding = jnp.zeros((abs(offset),) + array.shape[1:], array.dtype)
    if offset >= 0:
        return jnp.concatenate([array, padding], axis=0)[offset:offset + count]
    return jnp.concatenate([padding, array], axis=0)[:count]


def rounded(array):
    return lax.optimization_barrier(array.astype(jnp.bfloat16)).astype(jnp.float32)


def reference(queries, keys, values, out_grad, pair_mask):
    head_shape = (VIDEO_FRAMES, FTOK, HEADS, HDIM)
    query_heads = queries.reshape(head_shape).astype(jnp.float32)
    key_heads = keys.reshape(head_shape).astype(jnp.float32)
    value_heads = values.reshape(head_shape).astype(jnp.float32)
    grad_heads = out_grad.reshape(head_shape).astype(jnp.float32)
    score_scale = HDIM ** -0.5
    offsets = slot_offsets(DISTANCE_LEVELS)
    live_flags = pair_mask.astype(jnp.float32)[:, :, None, None, None]
    row_total = jnp.zeros((VIDEO_FRAMES, HEADS, FTOK), jnp.float32)
    numerator = jnp.zeros(head_shape, jnp.float32)
    for slot_index, offset in enumerate(offsets):
        key_near = frame_shifted(key_heads, offset)
        value_near = frame_shifted(value_heads, offset)
        scores = jnp.einsum("fqhd,fkhd->fhqk", query_heads, key_near) * score_scale
        attention_weights = jnp.exp(scores) * live_flags[:, slot_index]
        row_total = row_total + jnp.sum(attention_weights, axis=3)
        numerator = numerator + jnp.einsum("fhqk,fkhd->fqhd", rounded(attention_weights), value_near)
    forward_output = numerator / jnp.transpose(row_total, (0, 2, 1))[..., None]
    row_delta = jnp.transpose(jnp.sum(grad_heads * forward_output, axis=3), (0, 2, 1))
    query_sum = jnp.zeros(head_shape, jnp.float32)
    key_sum = jnp.zeros(head_shape, jnp.float32)
    value_sum = jnp.zeros(head_shape, jnp.float32)
    for slot_index, offset in enumerate(offsets):
        key_near = frame_shifted(key_heads, offset)
        value_near = frame_shifted(value_heads, offset)
        scores = jnp.einsum("fqhd,fkhd->fhqk", query_heads, key_near) * score_scale
        probabilities = jnp.exp(scores) * live_flags[:, slot_index] / row_total[..., None]
        dprobs = jnp.einsum("fqhd,fkhd->fhqk", grad_heads, value_near)
        dscores = rounded(probabilities * (dprobs - row_delta[..., None]))
        query_sum = query_sum + jnp.einsum("fhqk,fkhd->fqhd", dscores, key_near)
        key_part = rounded(jnp.einsum("fhqk,fqhd->fkhd", dscores, query_heads) * score_scale)
        value_part = rounded(jnp.einsum("fhqk,fqhd->fkhd", rounded(probabilities), grad_heads))
        key_sum = key_sum + frame_shifted(key_part, -offset)
        value_sum = value_sum + frame_shifted(value_part, -offset)
    flat_shape = (TOKENS, HEADS * HDIM)
    query_grad = (query_sum * score_scale).astype(jnp.bfloat16).reshape(flat_shape)
    key_grad = key_sum.astype(jnp.bfloat16).reshape(flat_shape)
    value_grad = value_sum.astype(jnp.bfloat16).reshape(flat_shape)
    return query_grad, key_grad, value_grad
```

```python
import functools
import math

import jax
import jax.numpy as jnp
from jax import lax
from jax.experimental import pallas as pl
from jax.experimental.pallas import tpu as pltpu
from jax.sharding import PartitionSpec as P

HDIM = 128
SLOT_OF_OFFSET = {0: 0, 1: 1, -1: 2, 2: 3, -2: 4}
NT = (((1,), (1,)), ((), ()))
TN = (((0,), (0,)), ((), ()))
MESH = pl.DeviceIdType.MESH


def dot(a, b, dims=(((1,), (0,)), ((), ()))):
    return lax.dot_general(a, b, dims, preferred_element_type=jnp.float32)


def kernel(
    half,
    pairs,
    mask_ref,
    q_ref,
    k_ref,
    v_ref,
    g_ref,
    dq_ref,
    dk_ref,
    dv_ref,
    kv,
    qg,
    ret,
    got,
    acc,
    dqs,
    fin,
    wbuf,
    dpbuf,
    x_send,
    x_recv,
    z_send,
    z_recv,
    r_send,
    r_recv,
    o_send,
    o_recv,
):
    tm = lax.axis_index("tm")
    par = lax.rem(tm, 2)
    pair = lax.div(tm, 2)
    other = 1 - par
    partner = tm + 1 - 2 * par
    has_left = pair > 0
    has_right = pair < pairs - 1
    sides = ((0, has_left, tm - 2), (1, has_right, tm + 2))
    scale = HDIM**-0.5

    def cols(which, c):
        return pl.ds(pl.multiple_of((which * half + c) * HDIM, HDIM), HDIM)

    def remote(src, dst, send, recv, to):
        return pltpu.make_async_remote_copy(
            src_ref=src,
            dst_ref=dst,
            send_sem=send,
            recv_sem=recv,
            device_id={"tm": to},
            device_id_type=MESH,
        )

    def x_copy(c, n, frame):
        src = (k_ref, v_ref, q_ref, g_ref)[n].at[:, cols(other, c)]
        dst = kv.at[c, 2 + frame, n] if n < 2 else qg.at[c, frame, n - 2]
        return remote(src, dst, x_send.at[c, n], x_recv.at[c, n], partner)

    def z_copy(c, side, frame, to):
        return remote(
            kv.at[c, 2 + frame],
            kv.at[c, 4 * (1 - side) + frame],
            z_send.at[c, side, frame],
            z_recv.at[c, 1 - side, frame],
            to,
        )

    def z_arrival(c, side, frame):
        return remote(
            kv.at[c, 2 + frame],
            kv.at[c, 4 * side + frame],
            z_send.at[c, side, frame],
            z_recv.at[c, side, frame],
            partner,
        )

    def r_copy(c, side, to):
        return remote(
            ret.at[c, side],
            got.at[c, 1 - side],
            r_send.at[c, side],
            r_recv.at[c, 1 - side],
            to,
        )

    def r_arrival(c, side):
        return remote(
            ret.at[c, side], got.at[c, side], r_send.at[c, side], r_recv.at[c, side], partner
        )

    def o_copy(c, n, which):
        src = dqs.at[c, other] if n == 0 else fin.at[c, n - 1]
        dst = (dq_ref, dk_ref, dv_ref)[n].at[:, cols(which, c)]
        return remote(src, dst, o_send.at[c, n], o_recv.at[c, n], partner)

    barrier = pltpu.get_barrier_semaphore()
    pl.semaphore_signal(barrier, inc=1, device_id={"tm": partner}, device_id_type=MESH)
    for _, there, to in sides:

        @pl.when(there)
        def _():
            pl.semaphore_signal(barrier, inc=1, device_id={"tm": to}, device_id_type=MESH)

    def stage(c, carry):
        here = cols(par, c)
        kv[c, 2 + par, 0] = k_ref[:, here]
        kv[c, 2 + par, 1] = v_ref[:, here]
        qg[c, par, 0] = q_ref[:, here]
        qg[c, par, 1] = g_ref[:, here]
        return carry

    lax.fori_loop(0, half, stage, 0)

    for side, there, _ in sides:

        @pl.when(jnp.logical_not(there))
        def _():
            def clear(c, carry):
                kv[c, pl.ds(4 * side, 2)] = jnp.zeros((2,) + kv.shape[2:], kv.dtype)
                got[c, side] = jnp.zeros(got.shape[2:], got.dtype)
                return carry

            lax.fori_loop(0, half, clear, 0)

    pl.semaphore_wait(barrier, 1 + has_left.astype(jnp.int32) + has_right.astype(jnp.int32))

    def launch(c, carry):
        for n in range(4):
            x_copy(c, n, par).start()
        for side, there, to in sides:

            @pl.when(there)
            def _():
                z_copy(c, side, par, to).start()

        return carry

    lax.fori_loop(0, half, launch, 0)

    def forward(c):
        for n in range(2):
            x_copy(c, n, other).wait_recv()
        for side, there, to in sides:

            @pl.when(there)
            def _():
                z_copy(c, side, other, to).start()

    def compute(c):
        sums = []
        for f in range(2):
            q = qg[c, f, 0]
            g = qg[c, f, 1]
            total = jnp.zeros((1, q.shape[0]), jnp.float32)
            mixed = jnp.zeros((1, q.shape[0]), jnp.float32)
            for j in range(5):
                live = mask_ref[2 * pair + f, SLOT_OF_OFFSET[j - 2]].astype(jnp.float32)
                w = jnp.exp2(dot(kv[c, f + j, 0], q, NT) * (scale * math.log2(math.e))) * live
                dp = dot(kv[c, f + j, 1], g, NT)
                wbuf[f, j] = w
                dpbuf[f, j] = dp
                total = total + jnp.sum(w, axis=0, keepdims=True)
                mixed = mixed + jnp.sum(w * dp, axis=0, keepdims=True)
            inverse = 1.0 / total
            sums.append((inverse, mixed * inverse))
        dq = [None, None]
        for slot in range(6):
            dk = dv = None
            for f in range(2):
                j = slot - f
                if not 0 <= j < 5:
                    continue
                inverse, delta = sums[f]
                p = wbuf[f, j] * inverse
                ds = (p * (dpbuf[f, j] - delta)).astype(jnp.bfloat16)
                dv_term = dot(p.astype(jnp.bfloat16), qg[c, f, 1])
                dk_term = dot(ds, qg[c, f, 0])
                dq_term = dot(ds, kv[c, slot, 0], TN)
                dv = dv_term if dv is None else dv + dv_term
                dk = dk_term if dk is None else dk + dk_term
                dq[f] = dq_term if dq[f] is None else dq[f] + dq_term
            dk = dk * scale
            if 2 <= slot < 4:
                acc[c, slot - 2, 0] = dk
                acc[c, slot - 2, 1] = dv
            else:
                ret[c, slot // 4, slot % 2, 0] = dk.astype(jnp.bfloat16)
                ret[c, slot // 4, slot % 2, 1] = dv.astype(jnp.bfloat16)
        for f in range(2):
            dqs[c, f] = (dq[f] * scale).astype(jnp.bfloat16)

    def finish(c):
        for side, there, _ in sides:

            @pl.when(there)
            def _():
                r_arrival(c, side).wait_recv()

        def summed(frame, n):
            total = acc[c, frame, n]
            for side in range(2):
                total = total + got[c, side, frame, n].astype(jnp.float32)
            return total.astype(jnp.bfloat16)

        for n in range(2):
            fin[c, n] = summed(other, n)
            o_copy(c, n + 1, par).start()
        for n in range(2):
            (dk_ref, dv_ref)[n][:, cols(par, c)] = summed(par, n)

    ahead = min(2, half)
    for c in range(ahead):
        forward(c)

    def step(c, carry):
        @pl.when(c + ahead < half)
        def _():
            forward(c + ahead)

        for n in range(2, 4):
            x_copy(c, n, other).wait_recv()
        for side, there, _ in sides:

            @pl.when(there)
            def _():
                for frame in range(2):
                    z_arrival(c, side, frame).wait_recv()

        compute(c)
        for side, there, to in sides:

            @pl.when(there)
            def _():
                r_copy(c, side, to).start()

        o_copy(c, 0, par).start()
        dq_ref[:, cols(par, c)] = dqs[c, par]

        @pl.when(c >= 1)
        def _():
            finish(c - 1)

        return carry

    lax.fori_loop(0, half, step, 0)
    finish(half - 1)

    def drain(c, carry):
        for n in range(4):
            x_copy(c, n, par).wait_send()
        for side, there, to in sides:

            @pl.when(there)
            def _():
                for frame in range(2):
                    z_copy(c, side, frame, to).wait_send()
                r_copy(c, side, to).wait_send()

        for n in range(3):
            o_copy(c, n, par).wait_send()
            o_copy(c, n, other).wait_recv()
        return carry

    lax.fori_loop(0, half, drain, 0)


def shards(queries, keys, values, out_grad, pair_mask):
    rows, width = queries.shape
    half = width // HDIM // 2
    pairs = lax.axis_size("tm") // 2
    low, full = jnp.bfloat16, jnp.float32
    dma = pltpu.SemaphoreType.DMA
    flops = 2 * rows * rows * HDIM * 5 * 10 * half
    out = jax.ShapeDtypeStruct((rows, width), low)
    vmem = pl.BlockSpec(memory_space=pltpu.VMEM)
    return pl.pallas_call(
        functools.partial(kernel, half, pairs),
        out_shape=(out, out, out),
        in_specs=[pl.BlockSpec(memory_space=pltpu.SMEM)] + [vmem] * 4,
        out_specs=(vmem, vmem, vmem),
        scratch_shapes=[
            pltpu.VMEM((half, 6, 2, rows, HDIM), low),
            pltpu.VMEM((half, 2, 2, rows, HDIM), low),
            pltpu.VMEM((half, 2, 2, 2, rows, HDIM), low),
            pltpu.VMEM((half, 2, 2, 2, rows, HDIM), low),
            pltpu.VMEM((half, 2, 2, rows, HDIM), full),
            pltpu.VMEM((half, 2, rows, HDIM), low),
            pltpu.VMEM((half, 2, rows, HDIM), low),
            pltpu.VMEM((2, 5, rows, rows), full),
            pltpu.VMEM((2, 5, rows, rows), full),
            dma((half, 4)),
            dma((half, 4)),
            dma((half, 2, 2)),
            dma((half, 2, 2)),
            dma((half, 2)),
            dma((half, 2)),
            dma((half, 3)),
            dma((half, 3)),
        ],
        cost_estimate=pl.CostEstimate(
            flops=flops, bytes_accessed=14 * rows * width, transcendentals=10 * half * rows * rows
        ),
        compiler_params=pltpu.CompilerParams(
            collective_id=0, has_side_effects=True, vmem_limit_bytes=48 * 1024 * 1024
        ),
    )(pair_mask, queries, keys, values, out_grad)


def solution(mesh):
    split = P(("groups", "tm"), "head")
    return jax.shard_map(
        shards,
        mesh=mesh,
        in_specs=(split, split, split, split, P("groups", None)),
        out_specs=(split, split, split),
        check_vma=False,
    )
```

```python
import functools
import math

import jax
import jax.numpy as jnp
from jax import lax
from jax.experimental import pallas as pl
from jax.experimental.pallas import tpu as pltpu
from jax.sharding import PartitionSpec as P

HDIM = 128
SLOT_OF_OFFSET = {0: 0, 1: 1, -1: 2, 2: 3, -2: 4}
NT = (((1,), (1,)), ((), ()))
TN = (((0,), (0,)), ((), ()))
MESH = pl.DeviceIdType.MESH


def dot(a, b, dims=(((1,), (0,)), ((), ()))):
    return lax.dot_general(a, b, dims, preferred_element_type=jnp.float32)


def kernel(
    half,
    pairs,
    mask_ref,
    q_ref,
    k_ref,
    v_ref,
    g_ref,
    dq_ref,
    dk_ref,
    dv_ref,
    kv,
    qg,
    ret,
    got,
    acc,
    dqs,
    fin,
    wbuf,
    dpbuf,
    local,
    x_send,
    x_recv,
    z_send,
    z_recv,
    r_send,
    r_recv,
    o_send,
    o_recv,
):
    tm = lax.axis_index("tm")
    par = lax.rem(tm, 2)
    pair = lax.div(tm, 2)
    other = 1 - par
    partner = tm + 1 - 2 * par
    has_left = pair > 0
    has_right = pair < pairs - 1
    sides = ((0, has_left, tm - 2), (1, has_right, tm + 2))
    scale = HDIM**-0.5

    def cols(which, c):
        return pl.ds(pl.multiple_of((which * half + c) * HDIM, HDIM), HDIM)

    def remote(src, dst, send, recv, to):
        return pltpu.make_async_remote_copy(
            src_ref=src,
            dst_ref=dst,
            send_sem=send,
            recv_sem=recv,
            device_id={"tm": to},
            device_id_type=MESH,
        )

    def x_copy(c, n, frame):
        src = (k_ref, v_ref, q_ref, g_ref)[n].at[:, cols(other, c)]
        dst = kv.at[c, 2 + frame, n] if n < 2 else qg.at[c, frame, n - 2]
        return remote(src, dst, x_send.at[c, n], x_recv.at[c, n], partner)

    def z_copy(c, side, frame, to):
        return remote(
            kv.at[c, 2 + frame],
            kv.at[c, 4 * (1 - side) + frame],
            z_send.at[c, side, frame],
            z_recv.at[c, 1 - side, frame],
            to,
        )

    def z_arrival(c, side, frame):
        return remote(
            kv.at[c, 2 + frame],
            kv.at[c, 4 * side + frame],
            z_send.at[c, side, frame],
            z_recv.at[c, side, frame],
            partner,
        )

    def r_copy(c, side, to):
        return remote(
            ret.at[c, side],
            got.at[c, 1 - side],
            r_send.at[c, side],
            r_recv.at[c, 1 - side],
            to,
        )

    def r_arrival(c, side):
        return remote(
            ret.at[c, side], got.at[c, side], r_send.at[c, side], r_recv.at[c, side], partner
        )

    def o_copy(c, n, which):
        src = dqs.at[c, other] if n == 0 else fin.at[c, n - 1]
        dst = (dq_ref, dk_ref, dv_ref)[n].at[:, cols(which, c)]
        return remote(src, dst, o_send.at[c, n], o_recv.at[c, n], partner)

    barrier = pltpu.get_barrier_semaphore()
    pl.semaphore_signal(barrier, inc=1, device_id={"tm": partner}, device_id_type=MESH)
    for _, there, to in sides:

        @pl.when(there)
        def _():
            pl.semaphore_signal(barrier, inc=1, device_id={"tm": to}, device_id_type=MESH)

    def own_copy(c, n):
        src = (k_ref, v_ref, q_ref, g_ref)[n].at[:, cols(par, c)]
        dst = kv.at[c, 2 + par, n] if n < 2 else qg.at[c, par, n - 2]
        return pltpu.make_async_copy(src, dst, local.at[c, n])

    def stage(c, carry):
        for n in range(4):
            own_copy(c, n).start()
        return carry

    lax.fori_loop(0, half, stage, 0)

    for side, there, _ in sides:

        @pl.when(jnp.logical_not(there))
        def _():
            def clear(c, carry):
                kv[c, pl.ds(4 * side, 2)] = jnp.zeros((2,) + kv.shape[2:], kv.dtype)
                got[c, side] = jnp.zeros(got.shape[2:], got.dtype)
                return carry

            lax.fori_loop(0, half, clear, 0)

    pl.semaphore_wait(barrier, 1 + has_left.astype(jnp.int32) + has_right.astype(jnp.int32))

    def launch(c, carry):
        for n in range(4):
            x_copy(c, n, par).start()
        for n in range(2):
            own_copy(c, n).wait()
        for side, there, to in sides:

            @pl.when(there)
            def _():
                z_copy(c, side, par, to).start()

        return carry

    lax.fori_loop(0, half, launch, 0)

    def forward(c):
        for n in range(2):
            x_copy(c, n, other).wait_recv()
        for side, there, to in sides:

            @pl.when(there)
            def _():
                z_copy(c, side, other, to).start()

    def compute(c):
        sums = []
        for f in range(2):
            q = qg[c, f, 0]
            g = qg[c, f, 1]
            total = jnp.zeros((1, q.shape[0]), jnp.float32)
            mixed = jnp.zeros((1, q.shape[0]), jnp.float32)
            for j in range(5):
                live = mask_ref[2 * pair + f, SLOT_OF_OFFSET[j - 2]].astype(jnp.float32)
                w = jnp.exp2(dot(kv[c, f + j, 0], q, NT) * (scale * math.log2(math.e))) * live
                dp = dot(kv[c, f + j, 1], g, NT)
                wbuf[f, j] = w
                dpbuf[f, j] = dp
                total = total + jnp.sum(w, axis=0, keepdims=True)
                mixed = mixed + jnp.sum(w * dp, axis=0, keepdims=True)
            inverse = 1.0 / total
            sums.append((inverse, mixed * inverse))
        dq = [None, None]
        for slot in range(6):
            dk = dv = None
            for f in range(2):
                j = slot - f
                if not 0 <= j < 5:
                    continue
                inverse, delta = sums[f]
                p = wbuf[f, j] * inverse
                ds = (p * (dpbuf[f, j] - delta)).astype(jnp.bfloat16)
                dv_term = dot(p.astype(jnp.bfloat16), qg[c, f, 1])
                dk_term = dot(ds, qg[c, f, 0])
                dq_term = dot(ds, kv[c, slot, 0], TN)
                dv = dv_term if dv is None else dv + dv_term
                dk = dk_term if dk is None else dk + dk_term
                dq[f] = dq_term if dq[f] is None else dq[f] + dq_term
            dk = dk * scale
            if 2 <= slot < 4:
                acc[c, slot - 2, 0] = dk
                acc[c, slot - 2, 1] = dv
            else:
                ret[c, slot // 4, slot % 2, 0] = dk.astype(jnp.bfloat16)
                ret[c, slot // 4, slot % 2, 1] = dv.astype(jnp.bfloat16)
        for f in range(2):
            dqs[c, f] = (dq[f] * scale).astype(jnp.bfloat16)

    def finish(c):
        for side, there, _ in sides:

            @pl.when(there)
            def _():
                r_arrival(c, side).wait_recv()

        def summed(frame, n):
            total = acc[c, frame, n]
            for side in range(2):
                total = total + got[c, side, frame, n].astype(jnp.float32)
            return total.astype(jnp.bfloat16)

        for n in range(2):
            fin[c, n] = summed(other, n)
            o_copy(c, n + 1, par).start()
        for n in range(2):
            (dk_ref, dv_ref)[n][:, cols(par, c)] = summed(par, n)

    ahead = min(2, half)
    for c in range(ahead):
        forward(c)

    def step(c, carry):
        @pl.when(c + ahead < half)
        def _():
            forward(c + ahead)

        for n in range(2, 4):
            x_copy(c, n, other).wait_recv()
            own_copy(c, n).wait()
        for side, there, _ in sides:

            @pl.when(there)
            def _():
                for frame in range(2):
                    z_arrival(c, side, frame).wait_recv()

        compute(c)
        for side, there, to in sides:

            @pl.when(there)
            def _():
                r_copy(c, side, to).start()

        o_copy(c, 0, par).start()
        dq_ref[:, cols(par, c)] = dqs[c, par]

        @pl.when(c >= 1)
        def _():
            finish(c - 1)

        return carry

    lax.fori_loop(0, half, step, 0)
    finish(half - 1)

    def drain(c, carry):
        for n in range(4):
            x_copy(c, n, par).wait_send()
        for side, there, to in sides:

            @pl.when(there)
            def _():
                for frame in range(2):
                    z_copy(c, side, frame, to).wait_send()
                r_copy(c, side, to).wait_send()

        for n in range(3):
            o_copy(c, n, par).wait_send()
            o_copy(c, n, other).wait_recv()
        return carry

    lax.fori_loop(0, half, drain, 0)


def shards(queries, keys, values, out_grad, pair_mask):
    rows, width = queries.shape
    half = width // HDIM // 2
    pairs = lax.axis_size("tm") // 2
    low, full = jnp.bfloat16, jnp.float32
    dma = pltpu.SemaphoreType.DMA
    flops = 2 * rows * rows * HDIM * 5 * 10 * half
    out = jax.ShapeDtypeStruct((rows, width), low)
    vmem = pl.BlockSpec(memory_space=pltpu.VMEM)
    return pl.pallas_call(
        functools.partial(kernel, half, pairs),
        out_shape=(out, out, out),
        in_specs=[pl.BlockSpec(memory_space=pltpu.SMEM)] + [pl.BlockSpec(memory_space=pl.ANY)] * 4,
        out_specs=(vmem, vmem, vmem),
        scratch_shapes=[
            pltpu.VMEM((half, 6, 2, rows, HDIM), low),
            pltpu.VMEM((half, 2, 2, rows, HDIM), low),
            pltpu.VMEM((half, 2, 2, 2, rows, HDIM), low),
            pltpu.VMEM((half, 2, 2, 2, rows, HDIM), low),
            pltpu.VMEM((half, 2, 2, rows, HDIM), full),
            pltpu.VMEM((half, 2, rows, HDIM), low),
            pltpu.VMEM((half, 2, rows, HDIM), low),
            pltpu.VMEM((2, 5, rows, rows), full),
            pltpu.VMEM((2, 5, rows, rows), full),
            dma((half, 4)),
            dma((half, 4)),
            dma((half, 4)),
            dma((half, 2, 2)),
            dma((half, 2, 2)),
            dma((half, 2)),
            dma((half, 2)),
            dma((half, 3)),
            dma((half, 3)),
        ],
        cost_estimate=pl.CostEstimate(
            flops=flops, bytes_accessed=14 * rows * width, transcendentals=10 * half * rows * rows
        ),
        compiler_params=pltpu.CompilerParams(
            collective_id=0, has_side_effects=True, vmem_limit_bytes=60 * 1024 * 1024
        ),
    )(pair_mask, queries, keys, values, out_grad)


def solution(mesh):
    split = P(("groups", "tm"), "head")
    return jax.shard_map(
        shards,
        mesh=mesh,
        in_specs=(split, split, split, split, P("groups", None)),
        out_specs=(split, split, split),
        check_vma=False,
    )
```

```python
import functools
import math

import jax
import jax.numpy as jnp
from jax import lax
from jax.experimental import pallas as pl
from jax.experimental.pallas import tpu as pltpu
from jax.sharding import PartitionSpec as P

HDIM = 128
SLOT_OF_OFFSET = {0: 0, 1: 1, -1: 2, 2: 3, -2: 4}
NT = (((1,), (1,)), ((), ()))
TN = (((0,), (0,)), ((), ()))
MESH = pl.DeviceIdType.MESH


def dot(a, b, dims=(((1,), (0,)), ((), ()))):
    return lax.dot_general(a, b, dims, preferred_element_type=jnp.float32)


def kernel(
    half,
    pairs,
    mask_ref,
    q_ref,
    k_ref,
    v_ref,
    g_ref,
    dq_ref,
    dk_ref,
    dv_ref,
    near,
    kv,
    ret,
    got,
    acc,
    kvs,
    fin,
    own_part,
    part,
    part_in,
    stat,
    stat_in,
    wbuf,
    dpbuf,
    local,
    x_send,
    x_recv,
    z_send,
    z_recv,
    r_send,
    r_recv,
    p_send,
    p_recv,
    s_send,
    s_recv,
    o_send,
    o_recv,
):
    tm = lax.axis_index("tm")
    par = lax.rem(tm, 2)
    pair = lax.div(tm, 2)
    other = 1 - par
    partner = tm + 1 - 2 * par
    has_left = pair > 0
    has_right = pair < pairs - 1
    sides = ((0, has_left, tm - 2), (1, has_right, tm + 2))
    scale = HDIM**-0.5

    def cols(which, c):
        return pl.ds(pl.multiple_of((which * half + c) * HDIM, HDIM), HDIM)

    def remote(src, dst, send, recv, to):
        return pltpu.make_async_remote_copy(
            src_ref=src,
            dst_ref=dst,
            send_sem=send,
            recv_sem=recv,
            device_id={"tm": to},
            device_id_type=MESH,
        )

    sources = (q_ref, g_ref, k_ref, v_ref)

    def place(c, n, frame):
        return near.at[c, 2 + frame, n] if n < 2 else kv.at[c, frame, n - 2]

    def x_copy(c, n, frame):
        src = sources[n].at[:, cols(other, c)]
        return remote(src, place(c, n, frame), x_send.at[c, n], x_recv.at[c, n], partner)

    def z_copy(c, side, frame, to):
        return remote(
            near.at[c, 2 + frame],
            near.at[c, 4 * (1 - side) + frame],
            z_send.at[c, side, frame],
            z_recv.at[c, 1 - side, frame],
            to,
        )

    def z_arrival(c, side, frame):
        return remote(
            near.at[c, 2 + frame],
            near.at[c, 4 * side + frame],
            z_send.at[c, side, frame],
            z_recv.at[c, side, frame],
            partner,
        )

    def swap(src, dst, send, recv, c, side, to):
        return remote(
            src, dst.at[c, 1 - side], send.at[c, side], recv.at[c, 1 - side], to
        )

    def r_copy(c, side, to):
        return swap(ret.at[c, side], got, r_send, r_recv, c, side, to)

    def p_copy(c, side, to):
        return swap(part.at[c, side], part_in, p_send, p_recv, c, side, to)

    def s_copy(c, side, to):
        return swap(stat.at[c], stat_in, s_send, s_recv, c, side, to)

    def r_arrival(c, side):
        return remote(
            ret.at[c, side], got.at[c, side], r_send.at[c, side], r_recv.at[c, side], partner
        )

    def p_arrival(c, side):
        return remote(
            part.at[c, side], part_in.at[c, side], p_send.at[c, side], p_recv.at[c, side], partner
        )

    def s_arrival(c, side):
        return remote(
            stat.at[c], stat_in.at[c, side], s_send.at[c, side], s_recv.at[c, side], partner
        )

    def o_copy(c, n, which):
        src = fin.at[c] if n == 0 else kvs.at[c, other, n - 1]
        dst = (dq_ref, dk_ref, dv_ref)[n].at[:, cols(which, c)]
        return remote(src, dst, o_send.at[c, n], o_recv.at[c, n], partner)

    def each_side(act):
        for side, there, to in sides:

            @pl.when(there)
            def _():
                act(side, to)

    barrier = pltpu.get_barrier_semaphore()
    pl.semaphore_signal(barrier, inc=1, device_id={"tm": partner}, device_id_type=MESH)
    for _, there, to in sides:

        @pl.when(there)
        def _():
            pl.semaphore_signal(barrier, inc=1, device_id={"tm": to}, device_id_type=MESH)

    def own_copy(c, n):
        src = sources[n].at[:, cols(par, c)]
        return pltpu.make_async_copy(src, place(c, n, par), local.at[c, n])

    def stage(c, carry):
        for n in range(4):
            own_copy(c, n).start()
        return carry

    lax.fori_loop(0, half, stage, 0)

    for side, there, _ in sides:

        @pl.when(jnp.logical_not(there))
        def _():
            def clear(c, carry):
                near[c, pl.ds(4 * side, 2)] = jnp.zeros((2,) + near.shape[2:], near.dtype)
                got[c, side] = jnp.zeros(got.shape[2:], got.dtype)
                part_in[c, side] = jnp.zeros(part_in.shape[2:], part_in.dtype)
                stat_in[c, side] = jnp.zeros(stat_in.shape[2:], stat_in.dtype)
                return carry

            lax.fori_loop(0, half, clear, 0)

    pl.semaphore_wait(barrier, 1 + has_left.astype(jnp.int32) + has_right.astype(jnp.int32))

    def launch(c, carry):
        for n in range(4):
            x_copy(c, n, par).start()
        return carry

    lax.fori_loop(0, half, launch, 0)

    def send_own(c):
        for n in range(2):
            own_copy(c, n).wait()
        each_side(lambda side, to: z_copy(c, side, par, to).start())

    ahead = min(2, half)

    def forward(c):
        for n in range(2):
            x_copy(c, n, other).wait_recv()
        each_side(lambda side, to: z_copy(c, side, other, to).start())

        @pl.when(c + ahead < half)
        def _():
            send_own(c + ahead)

    for c in range(ahead):
        send_own(c)

    def first(c):
        now = lax.rem(c, 2)
        for slot in range(6):
            q = near[c, slot, 0]
            g = near[c, slot, 1]
            frame = lax.rem(2 * pair + 2 * pairs - 2 + slot, 2 * pairs)
            total = jnp.zeros((1, q.shape[0]), jnp.float32)
            mixed = jnp.zeros((1, q.shape[0]), jnp.float32)
            for f in range(2):
                j = slot - f
                if not 0 <= j < 5:
                    continue
                live = mask_ref[frame, SLOT_OF_OFFSET[2 - j]].astype(jnp.float32)
                w = jnp.exp2(dot(kv[c, f, 0], q, NT) * (scale * math.log2(math.e))) * live
                dp = dot(kv[c, f, 1], g, NT)
                wbuf[now, f, j] = w
                dpbuf[now, f, j] = dp
                total = total + jnp.sum(w, axis=0, keepdims=True)
                mixed = mixed + jnp.sum(w * dp, axis=0, keepdims=True)
            row = 2 * (slot % 2)
            if 2 <= slot < 4:
                own_part[c, row : row + 1] = total
                own_part[c, row + 1 : row + 2] = mixed
            else:
                part[c, slot // 4, row : row + 1] = total
                part[c, slot // 4, row + 1 : row + 2] = mixed

    def combine(c):
        each_side(lambda side, to: p_arrival(c, side).wait_recv())
        sums = own_part[c] + part_in[c, 0] + part_in[c, 1]
        for row in (0, 2):
            inverse = 1.0 / sums[row : row + 1]
            stat[c, row : row + 1] = inverse
            stat[c, row + 1 : row + 2] = sums[row + 1 : row + 2] * inverse
        each_side(lambda side, to: s_copy(c, side, to).start())

    def second(c):
        now = lax.rem(c, 2)
        each_side(lambda side, to: s_arrival(c, side).wait_recv())
        dk = [None, None]
        dv = [None, None]
        for slot in range(6):
            row = 2 * (slot % 2)
            held = stat[c] if 2 <= slot < 4 else stat_in[c, slot // 4]
            inverse = held[row : row + 1]
            delta = held[row + 1 : row + 2]
            q = near[c, slot, 0]
            g = near[c, slot, 1]
            dq = None
            for f in range(2):
                j = slot - f
                if not 0 <= j < 5:
                    continue
                p = wbuf[now, f, j] * inverse
                ds = (p * (dpbuf[now, f, j] - delta)).astype(jnp.bfloat16)
                dv_term = dot(p.astype(jnp.bfloat16), g)
                dk_term = dot(ds, q)
                dq_term = dot(ds, kv[c, f, 0], TN)
                dv[f] = dv_term if dv[f] is None else dv[f] + dv_term
                dk[f] = dk_term if dk[f] is None else dk[f] + dk_term
                dq = dq_term if dq is None else dq + dq_term
            dq = dq * scale
            if 2 <= slot < 4:
                acc[c, slot - 2] = dq
            else:
                ret[c, slot // 4, slot % 2] = dq.astype(jnp.bfloat16)
        each_side(lambda side, to: r_copy(c, side, to).start())
        for f in range(2):
            kvs[c, f, 0] = (dk[f] * scale).astype(jnp.bfloat16)
            kvs[c, f, 1] = dv[f].astype(jnp.bfloat16)
        for n in range(2):
            o_copy(c, n + 1, par).start()
        for n in range(2):
            (dk_ref, dv_ref)[n][:, cols(par, c)] = kvs[c, par, n]

    def finish(c):
        each_side(lambda side, to: r_arrival(c, side).wait_recv())

        def summed(frame):
            total = acc[c, frame]
            for side in range(2):
                total = total + got[c, side, frame].astype(jnp.float32)
            return total.astype(jnp.bfloat16)

        fin[c] = summed(other)
        o_copy(c, 0, par).start()
        dq_ref[:, cols(par, c)] = summed(par)

    forward(0)

    def step(c, carry):
        @pl.when(jnp.logical_and(c >= 1, c <= half))
        def _():
            combine(c - 1)

        @pl.when(c < half)
        def _():
            for n in range(2, 4):
                x_copy(c, n, other).wait_recv()
                own_copy(c, n).wait()
            for frame in range(2):
                each_side(lambda side, to: z_arrival(c, side, frame).wait_recv())
            first(c)
            each_side(lambda side, to: p_copy(c, side, to).start())

        @pl.when(c + 1 < half)
        def _():
            forward(c + 1)

        @pl.when(jnp.logical_and(c >= 1, c <= half))
        def _():
            second(c - 1)

        @pl.when(c >= 2)
        def _():
            finish(c - 2)

        return carry

    lax.fori_loop(0, half + 2, step, 0)

    def drain(c, carry):
        for n in range(4):
            x_copy(c, n, par).wait_send()

        def sent(side, to):
            for frame in range(2):
                z_copy(c, side, frame, to).wait_send()
            for copy in (r_copy, p_copy, s_copy):
                copy(c, side, to).wait_send()

        each_side(sent)
        for n in range(3):
            o_copy(c, n, par).wait_send()
            o_copy(c, n, other).wait_recv()
        return carry

    lax.fori_loop(0, half, drain, 0)


def shards(queries, keys, values, out_grad, pair_mask):
    rows, width = queries.shape
    half = width // HDIM // 2
    pairs = lax.axis_size("tm") // 2
    low, full = jnp.bfloat16, jnp.float32
    dma = pltpu.SemaphoreType.DMA
    flops = 2 * rows * rows * HDIM * 5 * 10 * half
    out = jax.ShapeDtypeStruct((rows, width), low)
    vmem = pl.BlockSpec(memory_space=pltpu.VMEM)
    return pl.pallas_call(
        functools.partial(kernel, half, pairs),
        out_shape=(out, out, out),
        in_specs=[pl.BlockSpec(memory_space=pltpu.SMEM)] + [pl.BlockSpec(memory_space=pl.ANY)] * 4,
        out_specs=(vmem, vmem, vmem),
        scratch_shapes=[
            pltpu.VMEM((half, 6, 2, rows, HDIM), low),
            pltpu.VMEM((half, 2, 2, rows, HDIM), low),
            pltpu.VMEM((half, 2, 2, rows, HDIM), low),
            pltpu.VMEM((half, 2, 2, rows, HDIM), low),
            pltpu.VMEM((half, 2, rows, HDIM), full),
            pltpu.VMEM((half, 2, 2, rows, HDIM), low),
            pltpu.VMEM((half, rows, HDIM), low),
            pltpu.VMEM((half, 4, rows), full),
            pltpu.VMEM((half, 2, 4, rows), full),
            pltpu.VMEM((half, 2, 4, rows), full),
            pltpu.VMEM((half, 4, rows), full),
            pltpu.VMEM((half, 2, 4, rows), full),
            pltpu.VMEM((2, 2, 5, rows, rows), full),
            pltpu.VMEM((2, 2, 5, rows, rows), full),
            dma((half, 4)),
            dma((half, 4)),
            dma((half, 4)),
            dma((half, 2, 2)),
            dma((half, 2, 2)),
            dma((half, 2)),
            dma((half, 2)),
            dma((half, 2)),
            dma((half, 2)),
            dma((half, 2)),
            dma((half, 2)),
            dma((half, 3)),
            dma((half, 3)),
        ],
        cost_estimate=pl.CostEstimate(
            flops=flops, bytes_accessed=14 * rows * width, transcendentals=10 * half * rows * rows
        ),
        compiler_params=pltpu.CompilerParams(
            collective_id=0, has_side_effects=True, vmem_limit_bytes=60 * 1024 * 1024
        ),
    )(pair_mask, queries, keys, values, out_grad)


def solution(mesh):
    split = P(("groups", "tm"), "head")
    return jax.shard_map(
        shards,
        mesh=mesh,
        in_specs=(split, split, split, split, P("groups", None)),
        out_specs=(split, split, split),
        check_vma=False,
    )
```

```python
import functools
import math

import jax
import jax.numpy as jnp
from jax import lax
from jax.experimental import pallas as pl
from jax.experimental.pallas import tpu as pltpu
from jax.sharding import PartitionSpec as P

HDIM = 128
SLOT_OF_OFFSET = {0: 0, 1: 1, -1: 2, 2: 3, -2: 4}
NT = (((1,), (1,)), ((), ()))
TN = (((0,), (0,)), ((), ()))
PIECES = 2
MESH = pl.DeviceIdType.MESH


def dot(a, b, dims=(((1,), (0,)), ((), ()))):
    return lax.dot_general(a, b, dims, preferred_element_type=jnp.float32)


def kernel(
    half,
    pairs,
    mask_ref,
    q_ref,
    k_ref,
    v_ref,
    g_ref,
    dq_ref,
    dk_ref,
    dv_ref,
    near,
    kv,
    ret,
    got,
    acc,
    kvs,
    fin,
    mine,
    own_part,
    part,
    part_in,
    stat,
    stat_in,
    wbuf,
    dpbuf,
    keep,
    local,
    x_send,
    x_recv,
    z_send,
    z_recv,
    r_send,
    r_recv,
    p_send,
    p_recv,
    s_send,
    s_recv,
    o_send,
    o_recv,
):
    tm = lax.axis_index("tm")
    par = lax.rem(tm, 2)
    pair = lax.div(tm, 2)
    other = 1 - par
    partner = tm + 1 - 2 * par
    has_left = pair > 0
    has_right = pair < pairs - 1
    sides = ((0, has_left, tm - 2), (1, has_right, tm + 2))
    scale = HDIM**-0.5

    def cols(which, c):
        return pl.ds(pl.multiple_of((which * half + c) * HDIM, HDIM), HDIM)

    def remote(src, dst, send, recv, to):
        return pltpu.make_async_remote_copy(
            src_ref=src,
            dst_ref=dst,
            send_sem=send,
            recv_sem=recv,
            device_id={"tm": to},
            device_id_type=MESH,
        )

    sources = (q_ref, g_ref, k_ref, v_ref)

    def place(c, n, frame):
        return near.at[c, 2 + frame, n] if n < 2 else kv.at[c, frame, n - 2]

    def x_copy(c, n, frame):
        src = sources[n].at[:, cols(other, c)]
        return remote(src, place(c, n, frame), x_send.at[c, n], x_recv.at[c, n], partner)

    def z_copy(c, side, frame, to):
        return remote(
            near.at[c, 2 + frame],
            near.at[c, 4 * (1 - side) + frame],
            z_send.at[c, side, frame],
            z_recv.at[c, 1 - side, frame],
            to,
        )

    def z_arrival(c, side, frame):
        return remote(
            near.at[c, 2 + frame],
            near.at[c, 4 * side + frame],
            z_send.at[c, side, frame],
            z_recv.at[c, side, frame],
            partner,
        )

    def swap(src, dst, send, recv, c, side, to):
        return remote(
            src, dst.at[c, 1 - side], send.at[c, side], recv.at[c, 1 - side], to
        )

    def r_copy(c, side, to):
        return swap(ret.at[c, side], got, r_send, r_recv, c, side, to)

    def p_copy(c, side, to):
        return swap(part.at[c, side], part_in, p_send, p_recv, c, side, to)

    def s_copy(c, side, to):
        return swap(stat.at[c], stat_in, s_send, s_recv, c, side, to)

    def r_arrival(c, side):
        return remote(
            ret.at[c, side], got.at[c, side], r_send.at[c, side], r_recv.at[c, side], partner
        )

    def p_arrival(c, side):
        return remote(
            part.at[c, side], part_in.at[c, side], p_send.at[c, side], p_recv.at[c, side], partner
        )

    def s_arrival(c, side):
        return remote(
            stat.at[c], stat_in.at[c, side], s_send.at[c, side], s_recv.at[c, side], partner
        )

    def o_copy(c, n, which):
        src = fin.at[c] if n == 0 else kvs.at[c, other, n - 1]
        dst = (dq_ref, dk_ref, dv_ref)[n].at[:, cols(which, c)]
        return remote(src, dst, o_send.at[c, n], o_recv.at[c, n], partner)

    def keep_copy(c, n):
        src = mine.at[c] if n == 0 else kvs.at[c, par, n - 1]
        dst = (dq_ref, dk_ref, dv_ref)[n].at[:, cols(par, c)]
        return pltpu.make_async_copy(src, dst, keep.at[c, n])

    def each_side(act):
        for side, there, to in sides:

            @pl.when(there)
            def _():
                act(side, to)

    barrier = pltpu.get_barrier_semaphore()
    pl.semaphore_signal(barrier, inc=1, device_id={"tm": partner}, device_id_type=MESH)
    for _, there, to in sides:

        @pl.when(there)
        def _():
            pl.semaphore_signal(barrier, inc=1, device_id={"tm": to}, device_id_type=MESH)

    def own_copy(c, n):
        src = sources[n].at[:, cols(par, c)]
        return pltpu.make_async_copy(src, place(c, n, par), local.at[c, n])

    def stage(c, carry):
        for n in range(4):
            own_copy(c, n).start()
        return carry

    lax.fori_loop(0, half, stage, 0)

    for side, there, _ in sides:

        @pl.when(jnp.logical_not(there))
        def _():
            def clear(c, carry):
                near[c, pl.ds(4 * side, 2)] = jnp.zeros((2,) + near.shape[2:], near.dtype)
                got[c, side] = jnp.zeros(got.shape[2:], got.dtype)
                part_in[c, side] = jnp.zeros(part_in.shape[2:], part_in.dtype)
                stat_in[c, side] = jnp.zeros(stat_in.shape[2:], stat_in.dtype)
                return carry

            lax.fori_loop(0, half, clear, 0)

    pl.semaphore_wait(barrier, 1 + has_left.astype(jnp.int32) + has_right.astype(jnp.int32))

    def launch(c, carry):
        for n in range(4):
            x_copy(c, n, par).start()
        return carry

    lax.fori_loop(0, half, launch, 0)

    def send_own(c):
        for n in range(2):
            own_copy(c, n).wait()
        each_side(lambda side, to: z_copy(c, side, par, to).start())

    ahead = min(2, half)

    def forward(c):
        for n in range(2):
            x_copy(c, n, other).wait_recv()
        each_side(lambda side, to: z_copy(c, side, other, to).start())

        @pl.when(c + ahead < half)
        def _():
            send_own(c + ahead)

    for c in range(ahead):
        send_own(c)

    def first(c):
        now = lax.rem(c, 2)
        for slot in range(6):
            q = near[c, slot, 0]
            g = near[c, slot, 1]
            frame = lax.rem(2 * pair + 2 * pairs - 2 + slot, 2 * pairs)
            total = jnp.zeros((1, q.shape[0]), jnp.float32)
            mixed = jnp.zeros((1, q.shape[0]), jnp.float32)
            for f in range(2):
                j = slot - f
                if not 0 <= j < 5:
                    continue
                live = mask_ref[frame, SLOT_OF_OFFSET[2 - j]].astype(jnp.float32)
                w = jnp.exp2(dot(kv[c, f, 0], q, NT) * (scale * math.log2(math.e))) * live
                dp = dot(kv[c, f, 1], g, NT)
                wbuf[now, f, j] = w
                dpbuf[now, f, j] = dp
                total = total + jnp.sum(w, axis=0, keepdims=True)
                mixed = mixed + jnp.sum(w * dp, axis=0, keepdims=True)
            row = 2 * (slot % 2)
            if 2 <= slot < 4:
                own_part[c, row : row + 1] = total
                own_part[c, row + 1 : row + 2] = mixed
            else:
                part[c, slot // 4, row : row + 1] = total
                part[c, slot // 4, row + 1 : row + 2] = mixed

    def combine(c):
        each_side(lambda side, to: p_arrival(c, side).wait_recv())
        sums = own_part[c] + part_in[c, 0] + part_in[c, 1]
        for row in (0, 2):
            inverse = 1.0 / sums[row : row + 1]
            stat[c, row : row + 1] = inverse
            stat[c, row + 1 : row + 2] = sums[row + 1 : row + 2] * inverse
        each_side(lambda side, to: s_copy(c, side, to).start())

    def second(c):
        now = lax.rem(c, 2)
        each_side(lambda side, to: s_arrival(c, side).wait_recv())
        dk = [None, None]
        dv = [None, None]
        for slot in range(6):
            row = 2 * (slot % 2)
            held = stat[c] if 2 <= slot < 4 else stat_in[c, slot // 4]
            inverse = held[row : row + 1]
            delta = held[row + 1 : row + 2]
            q = near[c, slot, 0]
            g = near[c, slot, 1]
            dq = None
            for f in range(2):
                j = slot - f
                if not 0 <= j < 5:
                    continue
                p = wbuf[now, f, j] * inverse
                ds = (p * (dpbuf[now, f, j] - delta)).astype(jnp.bfloat16)
                dv_term = dot(p.astype(jnp.bfloat16), g)
                dk_term = dot(ds, q)
                dq_term = dot(ds, kv[c, f, 0], TN)
                dv[f] = dv_term if dv[f] is None else dv[f] + dv_term
                dk[f] = dk_term if dk[f] is None else dk[f] + dk_term
                dq = dq_term if dq is None else dq + dq_term
            dq = dq * scale
            if 2 <= slot < 4:
                acc[c, slot - 2] = dq
            else:
                ret[c, slot // 4, slot % 2] = dq.astype(jnp.bfloat16)
        each_side(lambda side, to: r_copy(c, side, to).start())
        for f in range(2):
            kvs[c, f, 0] = (dk[f] * scale).astype(jnp.bfloat16)
            kvs[c, f, 1] = dv[f].astype(jnp.bfloat16)
        for n in range(2):
            o_copy(c, n + 1, par).start()
        for n in range(2):
            keep_copy(c, n + 1).start()

    def finish(c):
        each_side(lambda side, to: r_arrival(c, side).wait_recv())

        def summed(frame):
            total = acc[c, frame]
            for side in range(2):
                total = total + got[c, side, frame].astype(jnp.float32)
            return total.astype(jnp.bfloat16)

        fin[c] = summed(other)
        o_copy(c, 0, par).start()
        mine[c] = summed(par)
        keep_copy(c, 0).start()

    forward(0)

    def step(c, carry):
        @pl.when(jnp.logical_and(c >= 1, c <= half))
        def _():
            combine(c - 1)

        @pl.when(c < half)
        def _():
            for n in range(2, 4):
                x_copy(c, n, other).wait_recv()
                own_copy(c, n).wait()
            for frame in range(2):
                each_side(lambda side, to: z_arrival(c, side, frame).wait_recv())
            first(c)
            each_side(lambda side, to: p_copy(c, side, to).start())

        @pl.when(c + 1 < half)
        def _():
            forward(c + 1)

        @pl.when(jnp.logical_and(c >= 1, c <= half))
        def _():
            second(c - 1)

        @pl.when(c >= 2)
        def _():
            finish(c - 2)

        return carry

    lax.fori_loop(0, half + 2, step, 0)

    def drain(c, carry):
        for n in range(4):
            x_copy(c, n, par).wait_send()

        def sent(side, to):
            for frame in range(2):
                z_copy(c, side, frame, to).wait_send()
            for copy in (r_copy, p_copy, s_copy):
                copy(c, side, to).wait_send()

        each_side(sent)
        for n in range(3):
            o_copy(c, n, par).wait_send()
            o_copy(c, n, other).wait_recv()
            keep_copy(c, n).wait()
        return carry

    lax.fori_loop(0, half, drain, 0)


def deliver(*refs):
    *refs, held, arrive, sem = refs
    count = len(refs) // 2
    rows = refs[0].shape[0] // PIECES
    copies = []
    loads = []
    for n in range(count):
        for piece in range(PIECES):
            part = pl.ds(piece * rows, rows)
            here = held.at[n, part]
            loads.append(pltpu.make_async_copy(refs[n].at[part], here, arrive.at[n, piece]))
            copies.append(
                pltpu.make_async_copy(here, refs[count + n].at[part], sem.at[n, piece])
            )
    for load in loads:
        load.start()
    for load, copy in zip(loads, copies):
        load.wait()
        copy.start()
    for copy in copies:
        copy.wait()


def shards(queries, keys, values, out_grad, pair_mask):
    rows, width = queries.shape
    half = width // HDIM // 2
    pairs = lax.axis_size("tm") // 2
    low, full = jnp.bfloat16, jnp.float32
    dma = pltpu.SemaphoreType.DMA
    flops = 2 * rows * rows * HDIM * 5 * 10 * half
    out = jax.ShapeDtypeStruct((rows, width), low)
    results = pl.pallas_call(
        functools.partial(kernel, half, pairs),
        out_shape=(out, out, out),
        in_specs=[pl.BlockSpec(memory_space=pltpu.SMEM)] + [pl.BlockSpec(memory_space=pl.ANY)] * 4,
        out_specs=(pl.BlockSpec(memory_space=pl.ANY),) * 3,
        scratch_shapes=[
            pltpu.VMEM((half, 6, 2, rows, HDIM), low),
            pltpu.VMEM((half, 2, 2, rows, HDIM), low),
            pltpu.VMEM((half, 2, 2, rows, HDIM), low),
            pltpu.VMEM((half, 2, 2, rows, HDIM), low),
            pltpu.VMEM((half, 2, rows, HDIM), full),
            pltpu.VMEM((half, 2, 2, rows, HDIM), low),
            pltpu.VMEM((half, rows, HDIM), low),
            pltpu.VMEM((half, rows, HDIM), low),
            pltpu.VMEM((half, 4, rows), full),
            pltpu.VMEM((half, 2, 4, rows), full),
            pltpu.VMEM((half, 2, 4, rows), full),
            pltpu.VMEM((half, 4, rows), full),
            pltpu.VMEM((half, 2, 4, rows), full),
            pltpu.VMEM((2, 2, 5, rows, rows), full),
            pltpu.VMEM((2, 2, 5, rows, rows), full),
            dma((half, 3)),
            dma((half, 4)),
            dma((half, 4)),
            dma((half, 4)),
            dma((half, 2, 2)),
            dma((half, 2, 2)),
            dma((half, 2)),
            dma((half, 2)),
            dma((half, 2)),
            dma((half, 2)),
            dma((half, 2)),
            dma((half, 2)),
            dma((half, 3)),
            dma((half, 3)),
        ],
        cost_estimate=pl.CostEstimate(
            flops=flops, bytes_accessed=14 * rows * width, transcendentals=10 * half * rows * rows
        ),
        compiler_params=pltpu.CompilerParams(
            collective_id=0, has_side_effects=True, vmem_limit_bytes=60 * 1024 * 1024
        ),
    )(pair_mask, queries, keys, values, out_grad)
    anywhere = pl.BlockSpec(memory_space=pl.ANY)
    return pl.pallas_call(
        deliver,
        out_shape=(out, out, out),
        in_specs=[anywhere] * 3,
        out_specs=(pl.BlockSpec(memory_space=pl.ANY),) * 3,
        scratch_shapes=[
            pltpu.VMEM((3, rows, width), low),
            dma((3, PIECES)),
            dma((3, PIECES)),
        ],
        cost_estimate=pl.CostEstimate(
            flops=0, bytes_accessed=12 * rows * width, transcendentals=0
        ),
    )(*results)


def solution(mesh):
    split = P(("groups", "tm"), "head")
    return jax.shard_map(
        shards,
        mesh=mesh,
        in_specs=(split, split, split, split, P("groups", None)),
        out_specs=(split, split, split),
        check_vma=False,
    )
```

```python
import functools
import math

import jax
import jax.numpy as jnp
from jax import lax
from jax.experimental import pallas as pl
from jax.experimental.pallas import tpu as pltpu
from jax.sharding import PartitionSpec as P

HDIM = 128
SLOT_OF_OFFSET = {0: 0, 1: 1, -1: 2, 2: 3, -2: 4}
NT = (((1,), (1,)), ((), ()))
TN = (((0,), (0,)), ((), ()))
PIECES = 2
MESH = pl.DeviceIdType.MESH


def dot(a, b, dims=(((1,), (0,)), ((), ()))):
    return lax.dot_general(a, b, dims, preferred_element_type=jnp.float32)


def kernel(
    half,
    pairs,
    mask_ref,
    q_ref,
    k_ref,
    v_ref,
    g_ref,
    dq_ref,
    dk_ref,
    dv_ref,
    near,
    kv,
    ret,
    got,
    acc,
    kvs,
    fin,
    mine,
    own_part,
    part,
    part_in,
    stat,
    stat_in,
    wbuf,
    dpbuf,
    keep,
    local,
    x_send,
    x_recv,
    z_send,
    z_recv,
    r_send,
    r_recv,
    p_send,
    p_recv,
    s_send,
    s_recv,
    o_send,
    o_recv,
):
    tm = lax.axis_index("tm")
    par = lax.rem(tm, 2)
    pair = lax.div(tm, 2)
    other = 1 - par
    partner = tm + 1 - 2 * par
    has_left = pair > 0
    has_right = pair < pairs - 1
    sides = ((0, has_left, tm - 2), (1, has_right, tm + 2))
    scale = HDIM**-0.5

    def cols(which, c):
        return pl.ds(pl.multiple_of((which * half + c) * HDIM, HDIM), HDIM)

    def remote(src, dst, send, recv, to):
        return pltpu.make_async_remote_copy(
            src_ref=src,
            dst_ref=dst,
            send_sem=send,
            recv_sem=recv,
            device_id={"tm": to},
            device_id_type=MESH,
        )

    sources = (q_ref, g_ref, k_ref, v_ref)

    def place(c, n, frame):
        return near.at[c, 2 + frame, n] if n < 2 else kv.at[c, frame, n - 2]

    def x_copy(c, n, frame):
        src = sources[n].at[:, cols(other, c)]
        return remote(src, place(c, n, frame), x_send.at[c, n], x_recv.at[c, n], partner)

    def z_copy(c, side, frame, to):
        return remote(
            near.at[c, 2 + frame],
            near.at[c, 4 * (1 - side) + frame],
            z_send.at[c, side, frame],
            z_recv.at[c, 1 - side, frame],
            to,
        )

    def z_arrival(c, side, frame):
        return remote(
            near.at[c, 2 + frame],
            near.at[c, 4 * side + frame],
            z_send.at[c, side, frame],
            z_recv.at[c, side, frame],
            partner,
        )

    def swap(src, dst, send, recv, c, side, to):
        return remote(
            src, dst.at[c, 1 - side], send.at[c, side], recv.at[c, 1 - side], to
        )

    def r_copy(c, side, to):
        return swap(ret.at[c, side], got, r_send, r_recv, c, side, to)

    def p_copy(c, side, to):
        return swap(part.at[c, side], part_in, p_send, p_recv, c, side, to)

    def s_copy(c, side, to):
        return swap(stat.at[c], stat_in, s_send, s_recv, c, side, to)

    def r_arrival(c, side):
        return remote(
            ret.at[c, side], got.at[c, side], r_send.at[c, side], r_recv.at[c, side], partner
        )

    def p_arrival(c, side):
        return remote(
            part.at[c, side], part_in.at[c, side], p_send.at[c, side], p_recv.at[c, side], partner
        )

    def s_arrival(c, side):
        return remote(
            stat.at[c], stat_in.at[c, side], s_send.at[c, side], s_recv.at[c, side], partner
        )

    def o_copy(c, n, which):
        src = fin.at[c] if n == 0 else kvs.at[c, other, n - 1]
        dst = (dq_ref, dk_ref, dv_ref)[n].at[:, cols(which, c)]
        return remote(src, dst, o_send.at[c, n], o_recv.at[c, n], partner)

    def keep_copy(c, n):
        src = mine.at[c] if n == 0 else kvs.at[c, par, n - 1]
        dst = (dq_ref, dk_ref, dv_ref)[n].at[:, cols(par, c)]
        return pltpu.make_async_copy(src, dst, keep.at[c, n])

    def each_side(act):
        for side, there, to in sides:

            @pl.when(there)
            def _():
                act(side, to)

    barrier = pltpu.get_barrier_semaphore()
    pl.semaphore_signal(barrier, inc=1, device_id={"tm": partner}, device_id_type=MESH)
    for _, there, to in sides:

        @pl.when(there)
        def _():
            pl.semaphore_signal(barrier, inc=1, device_id={"tm": to}, device_id_type=MESH)

    def own_copy(c, n):
        src = sources[n].at[:, cols(par, c)]
        return pltpu.make_async_copy(src, place(c, n, par), local.at[c, n])

    def stage(c, carry):
        for n in range(4):
            own_copy(c, n).start()
        return carry

    lax.fori_loop(0, half, stage, 0)

    for side, there, _ in sides:

        @pl.when(jnp.logical_not(there))
        def _():
            def clear(c, carry):
                near[c, pl.ds(4 * side, 2)] = jnp.zeros((2,) + near.shape[2:], near.dtype)
                got[c, side] = jnp.zeros(got.shape[2:], got.dtype)
                part_in[c, side] = jnp.zeros(part_in.shape[2:], part_in.dtype)
                stat_in[c, side] = jnp.zeros(stat_in.shape[2:], stat_in.dtype)
                return carry

            lax.fori_loop(0, half, clear, 0)

    pl.semaphore_wait(barrier, 1 + has_left.astype(jnp.int32) + has_right.astype(jnp.int32))

    def launch(c, carry):
        for n in range(2):

            @pl.when(c < half)
            def _():
                x_copy(c, n, par).start()

        for n in range(2, 4):

            @pl.when(c >= 1)
            def _():
                x_copy(c - 1, n, par).start()

        return carry

    lax.fori_loop(0, half + 1, launch, 0)

    def send_own(c):
        for n in range(2):
            own_copy(c, n).wait()
        each_side(lambda side, to: z_copy(c, side, par, to).start())

    ahead = min(3, half)

    def forward(c):
        for n in range(2):
            x_copy(c, n, other).wait_recv()
        each_side(lambda side, to: z_copy(c, side, other, to).start())

        @pl.when(c + ahead < half)
        def _():
            send_own(c + ahead)

    for c in range(ahead):
        send_own(c)

    def first(c):
        now = lax.rem(c, 2)
        for slot in (0, 1, 4, 5, 2, 3):
            q = near[c, slot, 0]
            g = near[c, slot, 1]
            frame = lax.rem(2 * pair + 2 * pairs - 2 + slot, 2 * pairs)
            total = jnp.zeros((1, q.shape[0]), jnp.float32)
            mixed = jnp.zeros((1, q.shape[0]), jnp.float32)
            for f in range(2):
                j = slot - f
                if not 0 <= j < 5:
                    continue
                live = mask_ref[frame, SLOT_OF_OFFSET[2 - j]].astype(jnp.float32)
                w = jnp.exp2(dot(kv[c, f, 0], q, NT) * (scale * math.log2(math.e))) * live
                dp = dot(kv[c, f, 1], g, NT)
                wbuf[now, f, j] = w
                dpbuf[now, f, j] = dp
                total = total + jnp.sum(w, axis=0, keepdims=True)
                mixed = mixed + jnp.sum(w * dp, axis=0, keepdims=True)
            row = 2 * (slot % 2)
            if 2 <= slot < 4:
                own_part[c, row : row + 1] = total
                own_part[c, row + 1 : row + 2] = mixed
            else:
                part[c, slot // 4, row : row + 1] = total
                part[c, slot // 4, row + 1 : row + 2] = mixed
            if slot == 5:
                each_side(lambda side, to: p_copy(c, side, to).start())

    def combine(c):
        each_side(lambda side, to: p_arrival(c, side).wait_recv())
        sums = own_part[c] + part_in[c, 0] + part_in[c, 1]
        for row in (0, 2):
            inverse = 1.0 / sums[row : row + 1]
            stat[c, row : row + 1] = inverse
            stat[c, row + 1 : row + 2] = sums[row + 1 : row + 2] * inverse
        each_side(lambda side, to: s_copy(c, side, to).start())

    def second(c):
        now = lax.rem(c, 2)
        each_side(lambda side, to: s_arrival(c, side).wait_recv())
        dk = [None, None]
        dv = [None, None]
        for slot in (0, 1, 4, 5, 2, 3):
            row = 2 * (slot % 2)
            held = stat[c] if 2 <= slot < 4 else stat_in[c, slot // 4]
            inverse = held[row : row + 1]
            delta = held[row + 1 : row + 2]
            q = near[c, slot, 0]
            g = near[c, slot, 1]
            dq = None
            for f in range(2):
                j = slot - f
                if not 0 <= j < 5:
                    continue
                p = wbuf[now, f, j] * inverse
                ds = (p * (dpbuf[now, f, j] - delta)).astype(jnp.bfloat16)
                dv_term = dot(p.astype(jnp.bfloat16), g)
                dk_term = dot(ds, q)
                dq_term = dot(ds, kv[c, f, 0], TN)
                dv[f] = dv_term if dv[f] is None else dv[f] + dv_term
                dk[f] = dk_term if dk[f] is None else dk[f] + dk_term
                dq = dq_term if dq is None else dq + dq_term
            dq = dq * scale
            if 2 <= slot < 4:
                acc[c, slot - 2] = dq
            else:
                ret[c, slot // 4, slot % 2] = dq.astype(jnp.bfloat16)
            if slot == 5:
                each_side(lambda side, to: r_copy(c, side, to).start())
        for f in range(2):
            kvs[c, f, 0] = (dk[f] * scale).astype(jnp.bfloat16)
            kvs[c, f, 1] = dv[f].astype(jnp.bfloat16)
        for n in range(2):
            o_copy(c, n + 1, par).start()
        for n in range(2):
            keep_copy(c, n + 1).start()

    def finish(c):
        each_side(lambda side, to: r_arrival(c, side).wait_recv())

        def summed(frame):
            total = acc[c, frame]
            for side in range(2):
                total = total + got[c, side, frame].astype(jnp.float32)
            return total.astype(jnp.bfloat16)

        fin[c] = summed(other)
        o_copy(c, 0, par).start()
        mine[c] = summed(par)
        keep_copy(c, 0).start()

    forward(0)

    def step(c, carry):
        @pl.when(jnp.logical_and(c >= 1, c <= half))
        def _():
            combine(c - 1)

        @pl.when(c < half)
        def _():
            for n in range(2, 4):
                x_copy(c, n, other).wait_recv()
                own_copy(c, n).wait()
            for frame in range(2):
                each_side(lambda side, to: z_arrival(c, side, frame).wait_recv())
            first(c)

        @pl.when(c + 1 < half)
        def _():
            forward(c + 1)

        @pl.when(jnp.logical_and(c >= 1, c <= half))
        def _():
            second(c - 1)

        @pl.when(c >= 2)
        def _():
            finish(c - 2)

        return carry

    lax.fori_loop(0, half + 2, step, 0)

    def drain(c, carry):
        for n in range(4):
            x_copy(c, n, par).wait_send()

        def sent(side, to):
            for frame in range(2):
                z_copy(c, side, frame, to).wait_send()
            for copy in (r_copy, p_copy, s_copy):
                copy(c, side, to).wait_send()

        each_side(sent)
        for n in range(3):
            o_copy(c, n, par).wait_send()
            o_copy(c, n, other).wait_recv()
            keep_copy(c, n).wait()
        return carry

    lax.fori_loop(0, half, drain, 0)


def deliver(*refs):
    *refs, held, arrive, sem = refs
    count = len(refs) // 2
    rows = refs[0].shape[0] // PIECES
    copies = []
    loads = []
    for n in range(count):
        for piece in range(PIECES):
            part = pl.ds(piece * rows, rows)
            here = held.at[n, part]
            loads.append(pltpu.make_async_copy(refs[n].at[part], here, arrive.at[n, piece]))
            copies.append(
                pltpu.make_async_copy(here, refs[count + n].at[part], sem.at[n, piece])
            )
    for load in loads:
        load.start()
    for load, copy in zip(loads, copies):
        load.wait()
        copy.start()
    for copy in copies:
        copy.wait()


def shards(queries, keys, values, out_grad, pair_mask):
    rows, width = queries.shape
    half = width // HDIM // 2
    pairs = lax.axis_size("tm") // 2
    low, full = jnp.bfloat16, jnp.float32
    dma = pltpu.SemaphoreType.DMA
    flops = 2 * rows * rows * HDIM * 5 * 10 * half
    out = jax.ShapeDtypeStruct((rows, width), low)
    results = pl.pallas_call(
        functools.partial(kernel, half, pairs),
        out_shape=(out, out, out),
        in_specs=[pl.BlockSpec(memory_space=pltpu.SMEM)] + [pl.BlockSpec(memory_space=pl.ANY)] * 4,
        out_specs=(pl.BlockSpec(memory_space=pl.ANY),) * 3,
        scratch_shapes=[
            pltpu.VMEM((half, 6, 2, rows, HDIM), low),
            pltpu.VMEM((half, 2, 2, rows, HDIM), low),
            pltpu.VMEM((half, 2, 2, rows, HDIM), low),
            pltpu.VMEM((half, 2, 2, rows, HDIM), low),
            pltpu.VMEM((half, 2, rows, HDIM), full),
            pltpu.VMEM((half, 2, 2, rows, HDIM), low),
            pltpu.VMEM((half, rows, HDIM), low),
            pltpu.VMEM((half, rows, HDIM), low),
            pltpu.VMEM((half, 4, rows), full),
            pltpu.VMEM((half, 2, 4, rows), full),
            pltpu.VMEM((half, 2, 4, rows), full),
            pltpu.VMEM((half, 4, rows), full),
            pltpu.VMEM((half, 2, 4, rows), full),
            pltpu.VMEM((2, 2, 5, rows, rows), full),
            pltpu.VMEM((2, 2, 5, rows, rows), full),
            dma((half, 3)),
            dma((half, 4)),
            dma((half, 4)),
            dma((half, 4)),
            dma((half, 2, 2)),
            dma((half, 2, 2)),
            dma((half, 2)),
            dma((half, 2)),
            dma((half, 2)),
            dma((half, 2)),
            dma((half, 2)),
            dma((half, 2)),
            dma((half, 3)),
            dma((half, 3)),
        ],
        cost_estimate=pl.CostEstimate(
            flops=flops, bytes_accessed=14 * rows * width, transcendentals=10 * half * rows * rows
        ),
        compiler_params=pltpu.CompilerParams(
            collective_id=0, has_side_effects=True, vmem_limit_bytes=60 * 1024 * 1024
        ),
    )(pair_mask, queries, keys, values, out_grad)
    anywhere = pl.BlockSpec(memory_space=pl.ANY)
    return pl.pallas_call(
        deliver,
        out_shape=(out, out, out),
        in_specs=[anywhere] * 3,
        out_specs=(pl.BlockSpec(memory_space=pl.ANY),) * 3,
        scratch_shapes=[
            pltpu.VMEM((3, rows, width), low),
            dma((3, PIECES)),
            dma((3, PIECES)),
        ],
        cost_estimate=pl.CostEstimate(
            flops=0, bytes_accessed=12 * rows * width, transcendentals=0
        ),
    )(*results)


def solution(mesh):
    split = P(("groups", "tm"), "head")
    return jax.shard_map(
        shards,
        mesh=mesh,
        in_specs=(split, split, split, split, P("groups", None)),
        out_specs=(split, split, split),
        check_vma=False,
    )
```
